256 devices in a mesh: dp: 32 (over x, y, core), tp: 8 (over z).
Axes of the slice: x: 4, y: 4, z: 8, core: 2. Of those that a mesh axis runs over, the one named last changes fastest.
Arguments:
- tokens: bfloat16 [4096, 6144], P('dp'), may hold values from -6 to 6
- route_ids: int32 [4096, 2], P('dp'), may hold values from 0 to 3, all different within a row; in each aligned block of 128 rows (0 to 127, 128 to 255, ...) at most 72 rows name the same one
- route_weights: float32 [4096, 2], P('dp'), may hold values from 0.1 to 0.9
- grad_gate: bfloat16 [4096, 2, 8192], P('dp', None, 'tp'), may hold values from -1.1953125 to 1.1953125
- grad_up: bfloat16 [4096, 2, 8192], P('dp', None, 'tp'), may hold values from -1.1953125 to 1.1953125
- gate_weight: bfloat16 [24576, 8192], P('dp', 'tp'), may hold values from -0.078125 to 0.078125
- up_weight: bfloat16 [24576, 8192], P('dp', 'tp'), may hold values from -0.078125 to 0.078125
Outputs:
- grad_tokens: bfloat16 [4096, 6144], P('dp')
- grad_gate_weight: bfloat16 [24576, 8192], P('dp', 'tp')
- grad_up_weight: bfloat16 [24576, 8192], P('dp', 'tp')
The draws below stay inside these ranges and needn't reach their ends.
Inputs may be any that keep to these rules, and one draw needn't show every extreme that they name: `route_ids`: in each aligned block of 128 tokens (the tokens of one index of dp), no expert is named by more than 72 of the block's routes, a bound that some block reaches; a token's 2 ids differ.
All inputs are finite; a program needn't handle non-finite values.
Results may differ from the reference program's by a relative error of at most 0.0049.
Values may be sent and summed in bfloat16 or wider, within the bound.
No kernel may reach another device: no remote copies, remote signals or barrier semaphores. Data moves between devices by JAX's collectives and lax.ppermute only.
A program may use at most 128 MiB of HBM per device.

```python
import math
import jax
import jax.numpy as jnp
import numpy as np
from jax import lax

D = 6144
FF = 8192
EXPERTS = 4
TOP = 2
TOK_DEV = 128
CAP = 72
TOKENS = 4096
N_DP = 32


def steps_of(own_key, extent, pieces, low, top_value):
    def one(position, shards_of):
        heights = jax.random.uniform(jax.random.fold_in(jax.random.fold_in(own_key, 6), position), (shards_of,), jnp.float32, low / len(pieces), top_value / len(pieces))
        return jnp.repeat(jnp.exp(heights), extent[position] // shards_of).reshape((-1,) + (1,) * (len(extent) - position - 1))

    gain = one(*pieces[0])
    for cut in pieces[1:]:
        gain = gain * one(*cut)
    return gain


def shared_out(own_key, own, number, rows, amount, top, most, slope):
    order = jax.random.permutation(own_key, amount)
    heavy_load, ordinary = load_shares(amount, rows * top, most, slope, True), load_shares(amount, rows * top, most, slope, False)
    places = jnp.arange(amount)

    def named(sizes, turn):
        used = int((sizes > 0).sum())
        fixed = max(1, used // 4)
        passed = fixed + (places - fixed + turn * (used - fixed)) % max(1, amount - fixed)
        return jnp.zeros((amount,), jnp.int32).at[order[jnp.where(places < fixed, places, passed)]].set(jnp.asarray(sizes, jnp.int32))

    sizes = jnp.where(number % 4 == 0, named(heavy_load, number // 4), named(ordinary, number - number // 4 - 1))
    mixed = jax.random.permutation(jax.random.fold_in(own, 3), amount)
    source_of, sink = mixed[0:amount // 2 * 2:2], mixed[1:amount // 2 * 2:2]
    margin = jnp.minimum(sizes[source_of] - 1, most - sizes[sink]) // 2
    margin = jnp.where((source_of == order[0]) | (sink == order[0]) | (sizes[sink] == 0), 0, jnp.maximum(margin, 0))
    passed = jax.random.randint(jax.random.fold_in(own, 4), (amount // 2,), 0, 1 << 20) % (margin + 1)
    sizes = sizes.at[source_of].add(-passed).at[sink].add(passed)
    members = jnp.searchsorted(jnp.cumsum(sizes), jnp.arange(rows * top), side="right").astype(jnp.int32)
    listing = members.reshape(top, rows).T
    listing = listing[jax.random.permutation(jax.random.fold_in(own, 1), rows)]
    turn = jax.random.randint(jax.random.fold_in(own, 2), (rows, 1), 0, top)
    return jnp.take_along_axis(listing, (jnp.arange(top)[None, :] + turn) % top, axis=1)


def load_shares(amount, total, bound, skew, full):
    weights = [(1 << 20) // math.isqrt(grade ** skew) + 1 for grade in range(1, amount + 1)]
    largest = bound if full else min(bound, max(-(-total // amount), total * weights[0] // sum(weights)))
    least = 1 if total - largest >= amount - 1 else 0
    counts, spare = [largest] + [least] * (amount - 1), total - largest - least * (amount - 1)
    while spare > 0:
        candidates = [i for i in range(1, amount) if counts[i] < largest] or [i for i in range(1, amount) if counts[i] < bound]
        mass, remaining = sum([weights[i] for i in candidates]), spare
        for i in candidates:
            addition = min(bound - counts[i], max(1, remaining * weights[i] // mass), spare)
            counts[i] = counts[i] + addition
            spare = spare - addition
    return np.array(counts)


def bell_draw(stream_key, dims, deviation, most, cuts=(), held_as=jnp.bfloat16):
    factor_of = steps_of(stream_key, dims, cuts, -0.22, 0.18) if cuts else 1.0
    drawn = jax.random.normal(stream_key, dims, jnp.float32) * deviation * factor_of
    return jnp.minimum(jnp.maximum(drawn, -most), most).astype(held_as)


def setup_inputs(seed: int = 0) -> dict:
    key_of = jax.random.split(jax.random.key(seed), 8)
    tokens = bell_draw(key_of[0], (TOKENS, D), 1.0, 6.0, ((0, 32),))
    route_ids_keys = jax.random.split(jax.random.fold_in(key_of[1], 1), TOKENS // TOK_DEV)
    route_ids_turns = jax.random.permutation(jax.random.fold_in(key_of[1], 3), TOKENS // TOK_DEV)
    route_ids = jax.vmap(lambda own, number: shared_out(jax.random.fold_in(key_of[1], 2), own, number, TOK_DEV, EXPERTS, TOP, CAP, 1))(route_ids_keys, route_ids_turns).reshape((TOKENS, TOP))
    route_weights = jnp.clip(0.1 + 0.79999997 * jax.random.uniform(key_of[2], (TOKENS, TOP), jnp.float32) ** steps_of(key_of[2], (TOKENS, TOP), ((0, 32),), -0.2, 0.2), 0.1, 0.9)
    grad_gate = bell_draw(key_of[3], (TOKENS, TOP, FF), 0.2, 1.1953125, ((0, 32), (2, 8)))
    grad_up = bell_draw(key_of[4], (TOKENS, TOP, FF), 0.2, 1.1953125, ((0, 32), (2, 8)))
    gate_weight = bell_draw(key_of[5], (EXPERTS * D, FF), D ** -0.5, 0.078125, ((0, 32), (1, 8)))
    up_weight = bell_draw(key_of[6], (EXPERTS * D, FF), D ** -0.5, 0.078125, ((0, 32), (1, 8)))
    return dict(tokens=tokens, route_ids=route_ids, route_weights=route_weights, grad_gate=grad_gate, grad_up=grad_up, gate_weight=gate_weight, up_weight=up_weight)


def reference(tokens, route_ids, route_weights, grad_gate, grad_up, gate_weight, up_weight):
    flat_ids = route_ids.reshape(-1)
    route_scale = route_weights.reshape(-1, 1).astype(jnp.float32)
    scaled_gate = (grad_gate.reshape(TOKENS * TOP, FF).astype(jnp.float32) * route_scale).astype(jnp.bfloat16)
    scaled_up = (grad_up.reshape(TOKENS * TOP, FF).astype(jnp.float32) * route_scale).astype(jnp.bfloat16)
    limit = N_DP * CAP

    def per_expert(carry_grad, expert):
        ordering = jnp.argsort((flat_ids != expert).astype(jnp.int32), stable=True)[:limit]
        live_rows = flat_ids[ordering] == expert
        token_rows = jnp.where(live_rows[:, None], tokens[ordering // TOP], jnp.zeros((), jnp.bfloat16))
        gate_rows = jnp.where(live_rows[:, None], scaled_gate[ordering], jnp.zeros((), jnp.bfloat16))
        up_rows = jnp.where(live_rows[:, None], scaled_up[ordering], jnp.zeros((), jnp.bfloat16))
        start = (expert * D).astype(jnp.int32)
        gate_block = lax.dynamic_slice_in_dim(gate_weight, start, D, 0)
        up_block = lax.dynamic_slice_in_dim(up_weight, start, D, 0)
        gate_grad = jnp.dot(token_rows.T, gate_rows, preferred_element_type=jnp.float32).astype(jnp.bfloat16)
        up_grad = jnp.dot(token_rows.T, up_rows, preferred_element_type=jnp.float32).astype(jnp.bfloat16)
        partial_value = jnp.dot(gate_rows, gate_block.T, preferred_element_type=jnp.float32)
        partial_value = partial_value + jnp.dot(up_rows, up_block.T, preferred_element_type=jnp.float32)
        partial_value = jnp.where(live_rows[:, None], partial_value, jnp.zeros((), jnp.float32))
        carry_grad = carry_grad.at[ordering // TOP].add(partial_value)
        return carry_grad, (gate_grad, up_grad)

    start_grad = jnp.zeros((TOKENS, D), jnp.float32)
    summed, stacked = lax.scan(per_expert, start_grad, jnp.arange(EXPERTS, dtype=jnp.int32))
    grad_gate_weight = stacked[0].reshape(EXPERTS * D, FF)
    grad_up_weight = stacked[1].reshape(EXPERTS * D, FF)
    return summed.astype(jnp.bfloat16), grad_gate_weight, grad_up_weight
```

```python
import jax
import jax.numpy as jnp
from jax import lax
from jax.experimental import pallas as pl
from jax.experimental.pallas import tpu as pltpu
from jax.sharding import PartitionSpec as P

CAP = 72
NX, NY, NC, NZ = 4, 4, 2, 8
BF, F32, I32 = jnp.bfloat16, jnp.float32, jnp.int32
VM = pl.BlockSpec(memory_space=pltpu.VMEM)
SM = pl.BlockSpec(memory_space=pltpu.SMEM)
ANY = pl.BlockSpec(memory_space=pl.ANY)
LIMIT = 48 * 1024 * 1024


def dp_perm(move):
    pairs = []
    for x in range(NX):
        for y in range(NY):
            for c in range(NC):
                tx, ty, tc = move(x, y, c)
                pairs.append(((x * NY + y) * NC + c, (tx % NX * NY + ty % NY) * NC + tc % NC))
    return pairs


def x_shift(value, k):
    return lax.ppermute(value, "dp", dp_perm(lambda x, y, c: (x + k, y, c)))


def y_shift(value, k):
    return lax.ppermute(value, "dp", dp_perm(lambda x, y, c: (x, y + k, c)))


def c_swap(value):
    return lax.ppermute(value, "dp", dp_perm(lambda x, y, c: (x, y, c + 1)))


def z_shift(value, k):
    return lax.ppermute(value, "tp", [(i, (i + k) % NZ) for i in range(NZ)])


def swap_low_z(value):
    pairs = []
    for x in range(NX):
        for low in range(NY * NC):
            for z in range(NZ):
                pairs.append(((x * 8 + low) * NZ + z, (x * 8 + z) * NZ + low))
    return lax.ppermute(value, ("dp", "tp"), pairs)


def one_hot_slots(ids):
    n = ids.shape[1]
    tri = (
        lax.broadcasted_iota(I32, (n, n), 0) < lax.broadcasted_iota(I32, (n, n), 1)
    ).astype(F32).astype(BF)
    rank = lax.broadcasted_iota(I32, (8, n), 0)
    hot0 = (rank == ids[0:1, :]).astype(F32)
    hot1 = (rank == ids[1:2, :]).astype(F32)
    pos0 = jnp.dot(hot0.astype(BF), tri, preferred_element_type=F32)
    pos1 = jnp.dot(hot1.astype(BF), tri, preferred_element_type=F32)
    pos1 = pos1 + jnp.sum(hot0, axis=1, keepdims=True)
    slot = lax.broadcasted_iota(I32, (CAP, n), 0)
    pairs = []
    for e in range(NX):
        at0 = jnp.where(hot0[e : e + 1, :] > 0.5, pos0[e : e + 1, :], -1.0).astype(I32)
        at1 = jnp.where(hot1[e : e + 1, :] > 0.5, pos1[e : e + 1, :], -1.0).astype(I32)
        pairs.append(((slot == at0).astype(F32), (slot == at1).astype(F32)))
    return pairs


def dispatch_kernel(ids_ref, w_ref, gg_ref, gu_ref, *out_refs):
    hots = one_hot_slots(ids_ref[...])
    w = w_ref[...]
    ff = gg_ref.shape[2]
    for part, ref in enumerate((gg_ref, gu_ref)):
        s0 = (ref[:, 0, :].astype(F32) * w[:, 0:1]).astype(BF)
        s1 = (ref[:, 1, :].astype(F32) * w[:, 1:2]).astype(BF)
        for e in range(NX):
            d0, d1 = hots[e]
            rows = jnp.dot(d0.astype(BF), s0, preferred_element_type=F32)
            rows = rows + jnp.dot(d1.astype(BF), s1, preferred_element_type=F32)
            out_refs[e][:, part * ff : (part + 1) * ff] = rows.astype(BF)


def token_kernel(x_ref, ids_ref, tok_ref, dep_ref, out_ref):
    hots = one_hot_slots(ids_ref[...])
    slabs = NY * NC
    cols = tok_ref.shape[1] // slabs
    for k in range(NX):
        d = (hots[k][0] + hots[k][1]).astype(BF)
        base = lax.rem(x_ref[0] + k, NX) * slabs
        for g in range(slabs):
            rows = jnp.dot(d, tok_ref[:, g * cols : (g + 1) * cols], preferred_element_type=F32)
            out_ref[base + g] = rows.astype(BF)


def partial_kernel(o_ref, g_ref, u_ref, *refs):
    pieces, (p_ref, s_ref) = refs[:-2], refs[-2:]
    ff = g_ref.shape[1]
    cols = g_ref.shape[0]
    over = (((1,), (1,)), ((), ()))
    at = 0
    n = 4 * CAP
    for ref in pieces:
        s_ref[at : at + ref.shape[0], :] = ref[...]
        at += ref.shape[0]
    tile = 256
    for m in range(8):
        slot = o_ref[m]

        def step(t, _, m=m, slot=slot):
            c = pl.multiple_of(t * tile, tile)
            acc = lax.dot_general(
                s_ref[m * n : (m + 1) * n, 0:ff], g_ref[pl.ds(c, tile), :], over, preferred_element_type=F32
            )
            acc = acc + lax.dot_general(
                s_ref[m * n : (m + 1) * n, ff : 2 * ff], u_ref[pl.ds(c, tile), :], over, preferred_element_type=F32
            )
            p_ref[slot, :, pl.ds(c, tile)] = acc.astype(BF)
            return 0

        lax.fori_loop(0, cols // tile, step, 0)


def combine_kernel(ids_ref, *refs):
    pieces, out_ref = refs[:-1], refs[-1]
    hots = one_hot_slots(ids_ref[...])
    over = (((0,), (0,)), ((), ()))
    total = None
    for k in range(NX):
        d = (hots[k][0] + hots[k][1]).astype(BF)
        part = lax.dot_general(d, pieces[k][...], over, preferred_element_type=F32)
        total = part if total is None else total + part
    out_ref[...] = total.astype(BF)


def assemble_kernel(slab_ref, *refs):
    pieces, out_ref = refs[:-1], refs[-1]
    cols = pieces[0].shape[1]
    for i, ref in enumerate(pieces):
        at = pl.multiple_of(slab_ref[i] * cols, 128)
        out_ref[:, pl.ds(at, cols)] = ref[...]


def call(kernel, out_shape, in_specs, flops=0, nbytes=0):
    return pl.pallas_call(
        kernel,
        out_shape=out_shape,
        in_specs=in_specs,
        out_specs=jax.tree.map(lambda _: VM, out_shape),
        compiler_params=pltpu.CompilerParams(vmem_limit_bytes=LIMIT),
        cost_estimate=pl.CostEstimate(flops=flops, bytes_accessed=nbytes, transcendentals=0),
    )


def on_device(tokens, route_ids, route_weights, grad_gate, grad_up, gate_weight, up_weight):
    toks, width = tokens.shape
    cols, ff = gate_weight.shape
    dp, z = lax.axis_index("dp"), lax.axis_index("tp")
    x, y, c = dp // 8, dp // 2 % 4, dp % 2
    ids = lax.rem(route_ids.T - x + NX, NX)
    ids_back = swap_low_z(ids)
    sent = call(
        dispatch_kernel,
        [jax.ShapeDtypeStruct((CAP, 2 * ff), BF)] * NX,
        [VM] * 4,
        2 * NX * CAP * toks * 2 * 2 * ff,
        4 << 20,
    )(ids, route_weights, grad_gate, grad_up)
    own = jnp.concatenate([sent[0]] + [x_shift(sent[k], k) for k in range(1, NX)], axis=0)
    half = 2 * CAP
    up1, down1 = y_shift(own, 1), y_shift(own, -1)
    up2, down2 = y_shift(up1[:half], 1), y_shift(down1[half:], -1)
    pieces = [own, up1, down1, up2, down2]
    pieces = pieces + [c_swap(p) for p in pieces]
    places = [(0, 0), (3, 0), (1, 0), (2, 0), (0, 1), (3, 1), (1, 1), (2, 1)]
    low = jnp.stack([(y + j) % NY * NC + (c + i) % NC for j, i in places]).astype(I32)
    offset = lax.rem(low - z + NZ, NZ)
    chunks, s_all = call(
        partial_kernel,
        [jax.ShapeDtypeStruct((8, 4 * CAP, cols), BF), jax.ShapeDtypeStruct((32 * CAP, 2 * ff), BF)],
        [SM] + [VM] * 12,
        2 * 32 * CAP * 2 * ff * cols,
        24 << 20,
    )(offset, gate_weight, up_weight, *pieces)

    up, down = chunks[4], chunks[5]
    for o in (3, 2, 1):
        up = z_shift(up, 1)
        up = (up.astype(F32) + chunks[o].astype(F32)).astype(BF)
        if o > 1:
            down = z_shift(down, -1)
            down = (down.astype(F32) + chunks[9 - o].astype(F32)).astype(BF)
    up, down = z_shift(up, 1), z_shift(down, -1)
    summed = (up.astype(F32) + down.astype(F32) + chunks[0].astype(F32)).astype(BF)
    back = [x_shift(summed[k * CAP : (k + 1) * CAP], -k) if k else summed[:CAP] for k in range(NX)]
    mine = call(
        combine_kernel, jax.ShapeDtypeStruct((toks, cols), BF), [VM] * 5, 2 * NX * CAP * toks * cols, 1 << 20
    )(ids_back, *back)
    mine = swap_low_z(mine)
    parts, up, down = [mine], mine, mine
    for step in range(4):
        up = z_shift(up, 1)
        parts.append(up)
        if step < 3:
            down = z_shift(down, -1)
            parts.append(down)
    slab = jnp.stack([(z + d) % NZ for d in (0, -1, 1, -2, 2, -3, 3, -4)]).astype(I32)
    result = call(
        assemble_kernel, jax.ShapeDtypeStruct((toks, width), BF), [SM] + [VM] * 8, 0, 3 << 20
    )(slab, *parts)

    x_send = call(
        token_kernel,
        jax.ShapeDtypeStruct((32, CAP, cols), BF),
        [SM, VM, VM, ANY],
        2 * NX * CAP * toks * width,
        5 << 20,
    )(x.reshape(1).astype(I32), ids, tokens, pieces[3])
    x_recv = lax.all_to_all(x_send, "dp", split_axis=0, concat_axis=0, tiled=True)
    order = jnp.stack(
        [(x - k) % NX * 8 + low[m] for m in range(8) for k in range(NX)]
    ).astype(I32)
    x_rows = x_recv[order].reshape(32 * CAP, cols)
    over_rows = (((0,), (0,)), ((), ()))
    grad_gate_weight = lax.dot_general(
        x_rows, s_all[:, :ff], over_rows, preferred_element_type=F32
    ).astype(BF)
    grad_up_weight = lax.dot_general(
        x_rows, s_all[:, ff:], over_rows, preferred_element_type=F32
    ).astype(BF)
    return (result, grad_gate_weight, grad_up_weight)


def solution(mesh):
    return jax.shard_map(
        on_device,
        mesh=mesh,
        in_specs=(
            P("dp", None),
            P("dp", None),
            P("dp", None),
            P("dp", None, "tp"),
            P("dp", None, "tp"),
            P("dp", "tp"),
            P("dp", "tp"),
        ),
        out_specs=(P("dp", None), P("dp", "tp"), P("dp", "tp")),
        check_vma=False,
    )
```

```python
import functools

import jax
import jax.numpy as jnp
from jax import lax
from jax.experimental import pallas as pl
from jax.experimental.pallas import tpu as pltpu
from jax.sharding import PartitionSpec as P

CAP = 72
NX, NY, NC, NZ = 4, 4, 2, 8
BF, F32, I32 = jnp.bfloat16, jnp.float32, jnp.int32
VM = pl.BlockSpec(memory_space=pltpu.VMEM)
SM = pl.BlockSpec(memory_space=pltpu.SMEM)
ANY = pl.BlockSpec(memory_space=pl.ANY)


def dp_perm(move):
    pairs = []
    for x in range(NX):
        for y in range(NY):
            for c in range(NC):
                tx, ty, tc = move(x, y, c)
                pairs.append(((x * NY + y) * NC + c, (tx % NX * NY + ty % NY) * NC + tc % NC))
    return pairs


def x_shift(value, k):
    return lax.ppermute(value, "dp", dp_perm(lambda x, y, c: (x + k, y, c)))


def y_shift(value, k):
    return lax.ppermute(value, "dp", dp_perm(lambda x, y, c: (x, y + k, c)))


def c_swap(value):
    return lax.ppermute(value, "dp", dp_perm(lambda x, y, c: (x, y, c + 1)))


def z_shift(value, k):
    return lax.ppermute(value, "tp", [(i, (i + k) % NZ) for i in range(NZ)])


def give_back(value, k):
    pairs = []
    for x in range(NX):
        for y in range(NY):
            for c in range(NC):
                for z in range(NZ):
                    to = ((x - k) % NX * NY + (y + z // 2) % NY) * NC + c
                    pairs.append((((x * NY + y) * NC + c) * NZ + z, to * NZ + z))
    return lax.ppermute(value, ("dp", "tp"), pairs)


def after(value, *others):
    return lax.optimization_barrier((value, *others))[0]


def one_hot_slots(ids):
    n = ids.shape[1]
    tri = (
        lax.broadcasted_iota(I32, (n, n), 0) < lax.broadcasted_iota(I32, (n, n), 1)
    ).astype(F32).astype(BF)
    rank = lax.broadcasted_iota(I32, (8, n), 0)
    hot0 = (rank == ids[0:1, :]).astype(F32)
    hot1 = (rank == ids[1:2, :]).astype(F32)
    pos0 = jnp.dot(hot0.astype(BF), tri, preferred_element_type=F32)
    pos1 = jnp.dot(hot1.astype(BF), tri, preferred_element_type=F32)
    pos1 = pos1 + jnp.sum(hot0, axis=1, keepdims=True)
    slot = lax.broadcasted_iota(I32, (CAP, n), 0)
    pairs = []
    for e in range(NX):
        at0 = jnp.where(hot0[e : e + 1, :] > 0.5, pos0[e : e + 1, :], -1.0).astype(I32)
        at1 = jnp.where(hot1[e : e + 1, :] > 0.5, pos1[e : e + 1, :], -1.0).astype(I32)
        pairs.append(((slot == at0).astype(F32), (slot == at1).astype(F32)))
    return pairs


def dispatch_kernel(ids_ref, w_ref, gg_ref, gu_ref, *out_refs):
    hots = one_hot_slots(ids_ref[...])
    w = w_ref[...]
    ff = gg_ref.shape[2]
    for part, ref in enumerate((gg_ref, gu_ref)):
        s0 = (ref[:, 0, :].astype(F32) * w[:, 0:1]).astype(BF)
        s1 = (ref[:, 1, :].astype(F32) * w[:, 1:2]).astype(BF)
        for e in range(NX):
            d0, d1 = hots[e]
            rows = jnp.dot(d0.astype(BF), s0, preferred_element_type=F32)
            rows = rows + jnp.dot(d1.astype(BF), s1, preferred_element_type=F32)
            out_refs[e][:, part * ff : (part + 1) * ff] = rows.astype(BF)


def token_kernel(x_ref, ids_ref, tok_ref, out_ref):
    hots = one_hot_slots(ids_ref[...])
    slabs = NY * NC
    cols = tok_ref.shape[1] // slabs
    for k in range(NX):
        d = (hots[k][0] + hots[k][1]).astype(BF)
        base = lax.rem(x_ref[0] + k, NX) * slabs
        for g in range(slabs):
            rows = jnp.dot(d, tok_ref[:, g * cols : (g + 1) * cols], preferred_element_type=F32)
            out_ref[base + g] = rows.astype(BF)


def partial_kernel(o_ref, wo_ref, ws_ref, own, up1, down1, up2, down2, p_ref, s_ref, sems):
    cols, ff2 = wo_ref.shape
    ff = ff2 // 2
    n = p_ref.shape[1]
    moves = [
        (own, s_ref.at[pl.ds(0, n), :]),
        (down1, s_ref.at[pl.ds(n, n), :]),
        (up2, s_ref.at[pl.ds(2 * n, n), pl.ds(0, ff)]),
        (down2, s_ref.at[pl.ds(2 * n, n), pl.ds(ff, ff)]),
        (up1, s_ref.at[pl.ds(3 * n, n), :]),
    ]
    copies = [pltpu.make_async_copy(a, b, sems.at[i]) for i, (a, b) in enumerate(moves)]
    for copy in copies:
        copy.start()
    for copy in copies:
        copy.wait()
    over = (((1,), (1,)), ((), ()))
    for which, w_ref in enumerate((wo_ref, ws_ref)):
        acc = lax.dot_general(s_ref[...], w_ref[...], over, preferred_element_type=F32)
        for j in range(4):
            p_ref[o_ref[which * 4 + j]] = acc[j * n : (j + 1) * n, :].astype(BF)


def rows_kernel(order_ref, x_ref, xs_ref):
    cap = x_ref.shape[1]

    def put(m, _):
        pair = [x_ref[order_ref[2 * m + i]].astype(F32) for i in range(2)]
        rows = pl.ds(pl.multiple_of(m * (2 * cap), 16), 2 * cap)
        xs_ref[rows, :] = jnp.concatenate(pair, axis=0).astype(BF)
        return 0

    lax.fori_loop(0, x_ref.shape[0] // 2, put, 0)


def weight_kernel(part, x_ref, sa, sb, sc, sd, out_ref, s_ref, sems):
    ff = out_ref.shape[1]
    n = sa.shape[0]
    tile = ff // 2
    copies = []
    for t in range(2):
        for i, ref in enumerate((sa, sb, sc, sd)):
            src = ref.at[:, pl.ds(part * ff + t * tile, tile)]
            dst = s_ref.at[pl.ds(i * n, n), pl.ds(t * tile, tile)]
            copies.append(pltpu.make_async_copy(src, dst, sems.at[t * 4 + i]))
            copies[-1].start()
    over = (((0,), (0,)), ((), ()))
    for t in range(2):
        for copy in copies[4 * t : 4 * t + 4]:
            copy.wait()
        at = slice(t * tile, (t + 1) * tile)
        acc = lax.dot_general(x_ref[...], s_ref[:, at], over, preferred_element_type=F32)
        out_ref[:, at] = acc.astype(BF)


def weight_grad(x_rows, parts, part, ff):
    rows, cols = x_rows.shape
    return call(
        functools.partial(weight_kernel, part),
        jax.ShapeDtypeStruct((cols, ff), BF),
        [VM] + [ANY] * 4,
        2 * cols * rows * ff,
        10 << 20,
        [pltpu.VMEM((rows, ff), BF), pltpu.SemaphoreType.DMA((8,))],
        30,
    )(x_rows, *parts)


def combine_kernel(ids_ref, *refs):
    pieces, out_ref = refs[:-1], refs[-1]
    hots = one_hot_slots(ids_ref[...])
    over = (((0,), (0,)), ((), ()))
    total = None
    for k in range(NX):
        d = (hots[k][0] + hots[k][1]).astype(BF)
        part = lax.dot_general(d, pieces[k][...], over, preferred_element_type=F32)
        total = part if total is None else total + part
    out_ref[...] = total.astype(BF)


def assemble_kernel(slab_ref, *refs):
    pieces, out_ref = refs[:-1], refs[-1]
    cols = pieces[0].shape[1]
    for i, ref in enumerate(pieces):
        at = pl.multiple_of(slab_ref[i] * cols, 128)
        out_ref[:, pl.ds(at, cols)] = ref[...]


def call(kernel, out_shape, in_specs, flops=0, nbytes=0, scratch=(), mib=12):
    return pl.pallas_call(
        kernel,
        out_shape=out_shape,
        in_specs=in_specs,
        out_specs=jax.tree.map(lambda _: VM, out_shape),
        scratch_shapes=scratch,
        compiler_params=pltpu.CompilerParams(vmem_limit_bytes=mib << 20),
        cost_estimate=pl.CostEstimate(flops=flops, bytes_accessed=nbytes, transcendentals=0),
    )


def ring_sum(chunks):
    up, down, marks = chunks[4], chunks[5], []
    for o in (3, 2, 1):
        up = z_shift(up, 1)
        up = (up.astype(F32) + chunks[o].astype(F32)).astype(BF)
        marks.append(up)
        if o > 1:
            down = z_shift(down, -1)
            down = (down.astype(F32) + chunks[9 - o].astype(F32)).astype(BF)
    up, down = z_shift(up, 1), z_shift(down, -1)
    return (up.astype(F32) + down.astype(F32) + chunks[0].astype(F32)).astype(BF), marks


def on_device(tokens, route_ids, route_weights, grad_gate, grad_up, gate_weight, up_weight):
    toks, width = tokens.shape
    cols, ff = gate_weight.shape
    dp, z = lax.axis_index("dp"), lax.axis_index("tp")
    x, y, c = dp // 8, dp // 2 % 4, dp % 2
    ids = lax.rem(route_ids.T - x + NX, NX)
    sent = call(
        dispatch_kernel,
        [jax.ShapeDtypeStruct((CAP, 2 * ff), BF)] * NX,
        [VM] * 4,
        2 * NX * CAP * toks * 2 * 2 * ff,
        4 << 20,
    )(ids, route_weights, grad_gate, grad_up)
    shifted = [sent[0]] + [x_shift(sent[k], k) for k in range(1, NX)]

    x_send = call(
        token_kernel,
        jax.ShapeDtypeStruct((32, CAP, cols), BF),
        [SM, VM, VM],
        2 * NX * CAP * toks * width,
        5 << 20,
        mib=16,
    )(x.reshape(1).astype(I32), ids, tokens)

    groups = ((0, 1), (2, 3))
    rows_a = jnp.concatenate([shifted[0], shifted[1]], axis=0)
    up1_a, down1_a = y_shift(rows_a, 1), y_shift(rows_a, -1)
    w_own = jnp.concatenate([gate_weight, up_weight], axis=1)
    w_other = c_swap(w_own)
    rows_b = jnp.concatenate([shifted[2], shifted[3]], axis=0)
    half_up, half_down = up1_a[:, :ff], down1_a[:, ff:]
    rows_b = after(rows_b, half_up, half_down, w_other, x_send)
    up2_a, down2_a = y_shift(half_up, 1), y_shift(half_down, -1)
    up1_b, down1_b = y_shift(rows_b, 1), y_shift(rows_b, -1)

    place = jnp.stack([2 * j + (c + i) % 2 for i in range(2) for j in range(4)]).astype(I32)
    offset = lax.rem(place - z + NZ, NZ)
    n = 2 * CAP

    def product(*pieces):
        return call(
            partial_kernel,
            [jax.ShapeDtypeStruct((8, n, cols), BF), jax.ShapeDtypeStruct((4 * n, 2 * ff), BF)],
            [SM] + [VM] * 2 + [ANY] * 5,
            2 * 8 * n * 2 * ff * cols,
            12 << 20,
            [pltpu.SemaphoreType.DMA((5,))],
            24,
        )(offset, w_own, w_other, *pieces)

    chunks_a, s_a = product(rows_a, up1_a, down1_a, up2_a, down2_a)
    up1_b, down1_b = after(up1_b, chunks_a), after(down1_b, chunks_a)
    up2_b, down2_b = y_shift(up1_b[:, :ff], 1), y_shift(down1_b[:, ff:], -1)
    sum_a, marks = ring_sum(chunks_a)
    chunks_b, s_b = product(rows_b, up1_b, down1_b, up2_b, down2_b)
    sum_b, marks = ring_sum(chunks_b)
    other_a, other_b = c_swap(after(s_a, marks[0])), c_swap(after(s_b, marks[0]))
    back = []
    for group, summed in zip(groups, (sum_a, sum_b)):
        for i, k in enumerate(group):
            back.append(give_back(summed[i * CAP : (i + 1) * CAP], k))
    back[-1] = after(back[-1], other_a, other_b)
    mine = call(
        combine_kernel, jax.ShapeDtypeStruct((toks, cols), BF), [VM] * 5, 2 * NX * CAP * toks * cols, 1 << 20
    )(ids, *back)

    x_recv = lax.all_to_all(after(x_send, marks[0]), "dp", split_axis=0, concat_axis=0, tiled=True)
    order = jnp.stack(
        [
            (x - k) % NX * 8 + (y + j) % NY * 2 + (c + i) % 2
            for group in groups
            for i in range(2)
            for j in range(4)
            for k in group
        ]
    ).astype(I32)
    x_rows = call(
        rows_kernel,
        jax.ShapeDtypeStruct((32 * CAP, cols), BF),
        [SM, VM],
        0,
        7 << 20,
        mib=16,
    )(order, x_recv)
    parts = [s_a, other_a, s_b, other_b]
    grad_gate_weight = weight_grad(x_rows, parts, 0, ff)
    grad_up_weight = weight_grad(x_rows, parts, 1, ff)

    beside = [x_rows, grad_gate_weight, grad_up_weight]
    got, up, down = [mine], mine, mine
    for step in range(4):
        up = z_shift(up, 1)
        got.append(up)
        if step < 3:
            down = z_shift(down, -1)
            got.append(down)
            up, down = after(up, beside[step]), after(down, beside[step])
    slab = jnp.stack([(y - p // 2) % NY * 2 + p % 2 for p in [(z + d) % NZ for d in (0, -1, 1, -2, 2, -3, 3, -4)]])
    result = call(
        assemble_kernel,
        jax.ShapeDtypeStruct((toks, width), BF),
        [SM] + [VM] * 8,
        0,
        3 << 20,
    )(slab.astype(I32), *got)
    return (result, grad_gate_weight, grad_up_weight)


def solution(mesh):
    return jax.shard_map(
        on_device,
        mesh=mesh,
        in_specs=(
            P("dp", None),
            P("dp", None),
            P("dp", None),
            P("dp", None, "tp"),
            P("dp", None, "tp"),
            P("dp", "tp"),
            P("dp", "tp"),
        ),
        out_specs=(P("dp", None), P("dp", "tp"), P("dp", "tp")),
        check_vma=False,
    )
```

```python
import functools

import jax
import jax.numpy as jnp
from jax import lax
from jax.experimental import pallas as pl
from jax.experimental.pallas import tpu as pltpu
from jax.sharding import PartitionSpec as P

CAP = 72
NX, NY, NC, NZ = 4, 4, 2, 8
BF, F32, I32 = jnp.bfloat16, jnp.float32, jnp.int32
VM = pl.BlockSpec(memory_space=pltpu.VMEM)
SM = pl.BlockSpec(memory_space=pltpu.SMEM)
ANY = pl.BlockSpec(memory_space=pl.ANY)


def dp_perm(move):
    pairs = []
    for x in range(NX):
        for y in range(NY):
            for c in range(NC):
                tx, ty, tc = move(x, y, c)
                pairs.append(((x * NY + y) * NC + c, (tx % NX * NY + ty % NY) * NC + tc % NC))
    return pairs


def x_shift(value, k):
    return lax.ppermute(value, "dp", dp_perm(lambda x, y, c: (x + k, y, c)))


def y_shift(value, k):
    return lax.ppermute(value, "dp", dp_perm(lambda x, y, c: (x, y + k, c)))


def c_swap(value):
    return lax.ppermute(value, "dp", dp_perm(lambda x, y, c: (x, y, c + 1)))


def z_shift(value, k):
    return lax.ppermute(value, "tp", [(i, (i + k) % NZ) for i in range(NZ)])


def give_back(value, k):
    pairs = []
    for x in range(NX):
        for y in range(NY):
            for c in range(NC):
                for z in range(NZ):
                    to = ((x - k) % NX * NY + (y + z // 2) % NY) * NC + c
                    pairs.append((((x * NY + y) * NC + c) * NZ + z, to * NZ + z))
    return lax.ppermute(value, ("dp", "tp"), pairs)


def after(value, *others):
    return lax.optimization_barrier((value, *others))[0]


def one_hot_slots(ids):
    n = ids.shape[1]
    tri = (
        lax.broadcasted_iota(I32, (n, n), 0) < lax.broadcasted_iota(I32, (n, n), 1)
    ).astype(F32).astype(BF)
    rank = lax.broadcasted_iota(I32, (8, n), 0)
    hot0 = (rank == ids[0:1, :]).astype(F32)
    hot1 = (rank == ids[1:2, :]).astype(F32)
    pos0 = jnp.dot(hot0.astype(BF), tri, preferred_element_type=F32)
    pos1 = jnp.dot(hot1.astype(BF), tri, preferred_element_type=F32)
    pos1 = pos1 + jnp.sum(hot0, axis=1, keepdims=True)
    slot = lax.broadcasted_iota(I32, (CAP, n), 0)
    pairs = []
    for e in range(NX):
        at0 = jnp.where(hot0[e : e + 1, :] > 0.5, pos0[e : e + 1, :], -1.0).astype(I32)
        at1 = jnp.where(hot1[e : e + 1, :] > 0.5, pos1[e : e + 1, :], -1.0).astype(I32)
        pairs.append(((slot == at0).astype(F32), (slot == at1).astype(F32)))
    return pairs


def dispatch_kernel(ids_ref, w_ref, gg_ref, gu_ref, *out_refs):
    hots = one_hot_slots(ids_ref[...])
    w = w_ref[...].T
    ff = gg_ref.shape[2]
    for part, ref in enumerate((gg_ref, gu_ref)):
        s0 = (ref[:, 0, :].astype(F32) * w[:, 0:1]).astype(BF)
        s1 = (ref[:, 1, :].astype(F32) * w[:, 1:2]).astype(BF)
        for e in range(NX):
            d0, d1 = hots[e]
            rows = jnp.dot(d0.astype(BF), s0, preferred_element_type=F32)
            rows = rows + jnp.dot(d1.astype(BF), s1, preferred_element_type=F32)
            out_refs[e][:, part * ff : (part + 1) * ff] = rows.astype(BF)


def token_kernel(x_ref, ids_ref, tok_ref, out_ref):
    hots = one_hot_slots(ids_ref[...])
    slabs = NY * NC
    cols = tok_ref.shape[1] // slabs
    for k in range(NX):
        d = (hots[k][0] + hots[k][1]).astype(BF)
        base = lax.rem(x_ref[0] + k, NX) * slabs
        for g in range(slabs):
            rows = jnp.dot(d, tok_ref[:, g * cols : (g + 1) * cols], preferred_element_type=F32)
            out_ref[base + g] = rows.astype(BF)


def partial_kernel(o_ref, go_ref, uo_ref, gs_ref, us_ref, own, up1, down1, up2, down2, p_ref, s_ref):
    ff = go_ref.shape[1]
    n = p_ref.shape[1]
    s_ref[0:n, :] = own[...]
    s_ref[n : 2 * n, :] = down1[...]
    s_ref[2 * n : 3 * n, 0:ff] = up2[...]
    s_ref[2 * n : 3 * n, ff:] = down2[...]
    s_ref[3 * n :, :] = up1[...]
    over = (((1,), (1,)), ((), ()))
    for which, (g_ref, u_ref) in enumerate(((go_ref, uo_ref), (gs_ref, us_ref))):
        acc = lax.dot_general(s_ref[:, 0:ff], g_ref[...], over, preferred_element_type=F32)
        acc = acc + lax.dot_general(s_ref[:, ff:], u_ref[...], over, preferred_element_type=F32)
        for j in range(4):
            p_ref[o_ref[which * 4 + j]] = acc[j * n : (j + 1) * n, :].astype(BF)


def rows_kernel(order_ref, x_ref, xs_ref):
    cap = x_ref.shape[1]

    def put(m, _):
        pair = [x_ref[order_ref[2 * m + i]].astype(F32) for i in range(2)]
        rows = pl.ds(pl.multiple_of(m * (2 * cap), 16), 2 * cap)
        xs_ref[rows, :] = jnp.concatenate(pair, axis=0).astype(BF)
        return 0

    lax.fori_loop(0, x_ref.shape[0] // 2, put, 0)


def weight_kernel(part, x_ref, sa, sb, sc, sd, out_ref, s_ref, sems):
    ff = out_ref.shape[1]
    n = sa.shape[0]
    tile = ff // 2
    copies = []
    for t in range(2):
        for i, ref in enumerate((sa, sb, sc, sd)):
            src = ref.at[:, pl.ds(part * ff + t * tile, tile)]
            dst = s_ref.at[pl.ds(i * n, n), pl.ds(t * tile, tile)]
            copies.append(pltpu.make_async_copy(src, dst, sems.at[t * 4 + i]))
            copies[-1].start()
    over = (((0,), (0,)), ((), ()))
    for t in range(2):
        for copy in copies[4 * t : 4 * t + 4]:
            copy.wait()
        at = slice(t * tile, (t + 1) * tile)
        acc = lax.dot_general(x_ref[...], s_ref[:, at], over, preferred_element_type=F32)
        out_ref[:, at] = acc.astype(BF)


def weight_grad(x_rows, parts, part, ff):
    rows, cols = x_rows.shape
    return call(
        functools.partial(weight_kernel, part),
        jax.ShapeDtypeStruct((cols, ff), BF),
        [VM] + [ANY] * 4,
        2 * cols * rows * ff,
        10 << 20,
        [pltpu.VMEM((rows, ff), BF), pltpu.SemaphoreType.DMA((8,))],
        18,
    )(x_rows, *parts)


def combine_kernel(ids_ref, *refs):
    pieces, out_ref = refs[:-1], refs[-1]
    hots = one_hot_slots(ids_ref[...])
    over = (((0,), (0,)), ((), ()))
    total = None
    for k in range(NX):
        d = (hots[k][0] + hots[k][1]).astype(BF)
        part = lax.dot_general(d, pieces[k][...], over, preferred_element_type=F32)
        total = part if total is None else total + part
    out_ref[...] = total.astype(BF)


def assemble_kernel(slab_ref, *refs):
    pieces, out_ref = refs[:-1], refs[-1]
    cols = pieces[0].shape[1]
    for i, ref in enumerate(pieces):
        at = pl.multiple_of(slab_ref[i] * cols, 128)
        out_ref[:, pl.ds(at, cols)] = ref[...]


def call(kernel, out_shape, in_specs, flops=0, nbytes=0, scratch=(), mib=6):
    return pl.pallas_call(
        kernel,
        out_shape=out_shape,
        in_specs=in_specs,
        out_specs=jax.tree.map(lambda _: VM, out_shape),
        scratch_shapes=scratch,
        compiler_params=pltpu.CompilerParams(vmem_limit_bytes=mib << 20),
        cost_estimate=pl.CostEstimate(flops=flops, bytes_accessed=nbytes, transcendentals=0),
    )


def ring_sum(chunks, ties=((), (), (), ())):
    up, down, marks = chunks[4], chunks[5], []
    for i, o in enumerate((3, 2, 1, 0)):
        if ties[i]:
            up = after(up, *ties[i])
            down = after(down, *ties[i]) if i < 3 else down
        up = z_shift(up, 1)
        total = up.astype(F32) + chunks[o].astype(F32)
        if i < 2:
            down = z_shift(down, -1)
            down = (down.astype(F32) + chunks[9 - o].astype(F32)).astype(BF)
        elif i == 2:
            down = z_shift(down, -1)
        else:
            total = total + down.astype(F32)
        up = total.astype(BF)
        marks.append(up)
    return marks


def on_device(tokens, route_ids, route_weights, grad_gate, grad_up, gate_weight, up_weight):
    toks, width = tokens.shape
    cols, ff = gate_weight.shape
    dp, z = lax.axis_index("dp"), lax.axis_index("tp")
    x, y, c = dp // 8, dp // 2 % 4, dp % 2
    ids = lax.rem(route_ids.T - x + NX, NX)
    sent = call(
        dispatch_kernel,
        [jax.ShapeDtypeStruct((CAP, 2 * ff), BF)] * NX,
        [VM] * 4,
        2 * NX * CAP * toks * 2 * 2 * ff,
        4 << 20,
    )(ids, route_weights.T, grad_gate, grad_up)
    shifted = [sent[0]] + [x_shift(sent[k], k) for k in range(1, NX)]

    x_send = call(
        token_kernel,
        jax.ShapeDtypeStruct((32, CAP, cols), BF),
        [SM, VM, VM],
        2 * NX * CAP * toks * width,
        5 << 20,
        mib=10,
    )(x.reshape(1).astype(I32), ids, tokens)

    groups = ((0, 1), (2, 3))
    rows_a = jnp.concatenate([shifted[0], shifted[1]], axis=0)
    up1_a, down1_a = y_shift(rows_a, 1), y_shift(rows_a, -1)
    gate_other, up_other = c_swap(gate_weight), c_swap(up_weight)
    rows_b = jnp.concatenate([shifted[2], shifted[3]], axis=0)
    up1_a = after(up1_a, x_send)
    half_up, half_down = up1_a[:, :ff], down1_a[:, ff:]
    rows_b = after(rows_b, half_up, half_down, gate_other, up_other)
    up2_a, down2_a = y_shift(half_up, 1), y_shift(half_down, -1)
    up1_b, down1_b = y_shift(rows_b, 1), y_shift(rows_b, -1)

    place = jnp.stack([2 * j + (c + i) % 2 for i in range(2) for j in range(4)]).astype(I32)
    offset = lax.rem(place - z + NZ, NZ)
    n = 2 * CAP

    def product(where, *pieces):
        return call(
            partial_kernel,
            [jax.ShapeDtypeStruct((8, n, cols), BF), jax.ShapeDtypeStruct((4 * n, 2 * ff), BF)],
            [SM] + [VM] * 9,
            2 * 8 * n * 2 * ff * cols,
            12 << 20,
            mib=16,
        )(where, gate_weight, up_weight, gate_other, up_other, *pieces)

    chunks_a, s_a = product(after(offset, rows_b), rows_a, up1_a, down1_a, up2_a, down2_a)
    up1_b, down1_b = after(up1_b, chunks_a), after(down1_b, chunks_a)
    up2_b, down2_b = y_shift(up1_b[:, :ff], 1), y_shift(down1_b[:, ff:], -1)
    chunks_b, s_b = product(offset, rows_b, up1_b, down1_b, up2_b, down2_b)
    marks_a = ring_sum(chunks_a, ((), (up2_b, down2_b), (chunks_b,), ()))
    other_a = c_swap(after(s_a, marks_a[0]))
    other_b = c_swap(after(s_b, marks_a[2]))
    x_recv = lax.all_to_all(after(x_send, half_up), "dp", split_axis=0, concat_axis=0, tiled=True)
    order = jnp.stack(
        [
            (x - k) % NX * 8 + (y + j) % NY * 2 + (c + i) % 2
            for group in groups
            for i in range(2)
            for j in range(4)
            for k in group
        ]
    ).astype(I32)
    x_rows = call(
        rows_kernel,
        jax.ShapeDtypeStruct((32 * CAP, cols), BF),
        [SM, VM],
        0,
        7 << 20,
        mib=10,
    )(order, x_recv)
    marks_b = ring_sum(chunks_b, ((marks_a[1],), (marks_a[2], other_a), (marks_a[3], other_b, x_rows), ()))
    parts = [s_a, other_a, s_b, other_b]
    grad_gate_weight = weight_grad(x_rows, parts, 0, ff)
    grad_up_weight = weight_grad(x_rows, parts, 1, ff)
    back = []
    for group, summed in zip(groups, (marks_a[3], after(marks_b[3], grad_gate_weight))):
        for i, k in enumerate(group):
            back.append(give_back(summed[i * CAP : (i + 1) * CAP], k))
    back[-1] = after(back[-1], grad_up_weight)
    mine = call(
        combine_kernel, jax.ShapeDtypeStruct((toks, cols), BF), [VM] * 5, 2 * NX * CAP * toks * cols, 1 << 20
    )(ids, *back)

    got, up, down = [mine], mine, mine
    for step in range(4):
        up = z_shift(up, 1)
        got.append(up)
        if step < 3:
            down = z_shift(down, -1)
            got.append(down)
    slab = jnp.stack([(y - p // 2) % NY * 2 + p % 2 for p in [(z + d) % NZ for d in (0, -1, 1, -2, 2, -3, 3, -4)]])
    result = call(
        assemble_kernel,
        jax.ShapeDtypeStruct((toks, width), BF),
        [SM] + [VM] * 8,
        0,
        3 << 20,
    )(slab.astype(I32), *got)
    return (result, grad_gate_weight, grad_up_weight)


def solution(mesh):
    return jax.shard_map(
        on_device,
        mesh=mesh,
        in_specs=(
            P("dp", None),
            P("dp", None),
            P("dp", None),
            P("dp", None, "tp"),
            P("dp", None, "tp"),
            P("dp", "tp"),
            P("dp", "tp"),
        ),
        out_specs=(P("dp", None), P("dp", "tp"), P("dp", "tp")),
        check_vma=False,
    )
```

```python
import functools

import jax
import jax.numpy as jnp
from jax import lax
from jax.experimental import pallas as pl
from jax.experimental.pallas import tpu as pltpu
from jax.sharding import PartitionSpec as P

CAP = 72
NX, NY, NC, NZ = 4, 4, 2, 8
BF, F32, I32 = jnp.bfloat16, jnp.float32, jnp.int32
VM = pl.BlockSpec(memory_space=pltpu.VMEM)
SM = pl.BlockSpec(memory_space=pltpu.SMEM)
ANY = pl.BlockSpec(memory_space=pl.ANY)


def dp_perm(move):
    pairs = []
    for x in range(NX):
        for y in range(NY):
            for c in range(NC):
                tx, ty, tc = move(x, y, c)
                pairs.append(((x * NY + y) * NC + c, (tx % NX * NY + ty % NY) * NC + tc % NC))
    return pairs


def x_shift(value, k):
    return lax.ppermute(value, "dp", dp_perm(lambda x, y, c: (x + k, y, c)))


def y_shift(value, k):
    return lax.ppermute(value, "dp", dp_perm(lambda x, y, c: (x, y + k, c)))


def c_swap(value):
    return lax.ppermute(value, "dp", dp_perm(lambda x, y, c: (x, y, c + 1)))


def z_shift(value, k):
    return lax.ppermute(value, "tp", [(i, (i + k) % NZ) for i in range(NZ)])


def give_back(value, k):
    pairs = []
    for x in range(NX):
        for y in range(NY):
            for c in range(NC):
                for z in range(NZ):
                    to = ((x - k) % NX * NY + (y + z // 2) % NY) * NC + c
                    pairs.append((((x * NY + y) * NC + c) * NZ + z, to * NZ + z))
    return lax.ppermute(value, ("dp", "tp"), pairs)


def after(value, *others):
    return lax.optimization_barrier((value, *others))[0]


def one_hot_slots(ids):
    n = ids.shape[1]
    tri = (
        lax.broadcasted_iota(I32, (n, n), 0) < lax.broadcasted_iota(I32, (n, n), 1)
    ).astype(F32).astype(BF)
    rank = lax.broadcasted_iota(I32, (8, n), 0)
    hot0 = (rank == ids[0:1, :]).astype(F32)
    hot1 = (rank == ids[1:2, :]).astype(F32)
    pos0 = jnp.dot(hot0.astype(BF), tri, preferred_element_type=F32)
    pos1 = jnp.dot(hot1.astype(BF), tri, preferred_element_type=F32)
    pos1 = pos1 + jnp.sum(hot0, axis=1, keepdims=True)
    slot = lax.broadcasted_iota(I32, (CAP, n), 0)
    pairs = []
    for e in range(NX):
        at0 = jnp.where(hot0[e : e + 1, :] > 0.5, pos0[e : e + 1, :], -1.0).astype(I32)
        at1 = jnp.where(hot1[e : e + 1, :] > 0.5, pos1[e : e + 1, :], -1.0).astype(I32)
        pairs.append(((slot == at0).astype(F32), (slot == at1).astype(F32)))
    return pairs


def dispatch_kernel(ids_ref, w_ref, gg_ref, gu_ref, *out_refs):
    hots = one_hot_slots(ids_ref[...])
    w = w_ref[...].T
    ff = gg_ref.shape[2]
    for part, ref in enumerate((gg_ref, gu_ref)):
        s0 = (ref[:, 0, :].astype(F32) * w[:, 0:1]).astype(BF)
        s1 = (ref[:, 1, :].astype(F32) * w[:, 1:2]).astype(BF)
        for e in range(NX):
            d0, d1 = hots[e]
            rows = jnp.dot(d0.astype(BF), s0, preferred_element_type=F32)
            rows = rows + jnp.dot(d1.astype(BF), s1, preferred_element_type=F32)
            out_refs[e][:, part * ff : (part + 1) * ff] = rows.astype(BF)


def token_kernel(x_ref, ids_ref, tok_ref, out_ref):
    hots = one_hot_slots(ids_ref[...])
    slabs = NY * NC
    cols = tok_ref.shape[1] // slabs
    for k in range(NX):
        d = (hots[k][0] + hots[k][1]).astype(BF)
        base = lax.rem(x_ref[0] + k, NX) * slabs
        for g in range(slabs):
            rows = jnp.dot(d, tok_ref[:, g * cols : (g + 1) * cols], preferred_element_type=F32)
            out_ref[base + g] = rows.astype(BF)


def partial_kernel(o_ref, go_ref, uo_ref, gs_ref, us_ref, own, up1, down1, up2, down2, p_ref, s_ref):
    ff = go_ref.shape[1]
    n = p_ref.shape[1]
    s_ref[0:n, :] = own[...]
    s_ref[n : 2 * n, :] = down1[...]
    s_ref[2 * n : 3 * n, 0:ff] = up2[...]
    s_ref[2 * n : 3 * n, ff:] = down2[...]
    s_ref[3 * n :, :] = up1[...]
    over = (((1,), (1,)), ((), ()))
    for which, (g_ref, u_ref) in enumerate(((go_ref, uo_ref), (gs_ref, us_ref))):
        acc = lax.dot_general(s_ref[:, 0:ff], g_ref[...], over, preferred_element_type=F32)
        acc = acc + lax.dot_general(s_ref[:, ff:], u_ref[...], over, preferred_element_type=F32)
        for j in range(4):
            p_ref[o_ref[which * 4 + j]] = acc[j * n : (j + 1) * n, :].astype(BF)


def rows_kernel(order_ref, x_ref, xs_ref):
    cap = x_ref.shape[1]

    def put(m, _):
        pair = [x_ref[order_ref[2 * m + i]].astype(F32) for i in range(2)]
        rows = pl.ds(pl.multiple_of(m * (2 * cap), 16), 2 * cap)
        xs_ref[rows, :] = jnp.concatenate(pair, axis=0).astype(BF)
        return 0

    lax.fori_loop(0, x_ref.shape[0] // 2, put, 0)


def weight_kernel(part, x_ref, sa, sb, sc, sd, out_ref, s_ref, sems):
    ff = out_ref.shape[1]
    n = sa.shape[0]
    tile = ff // 2
    copies = []
    for t in range(2):
        for i, ref in enumerate((sa, sb, sc, sd)):
            src = ref.at[:, pl.ds(part * ff + t * tile, tile)]
            dst = s_ref.at[pl.ds(i * n, n), pl.ds(t * tile, tile)]
            copies.append(pltpu.make_async_copy(src, dst, sems.at[t * 4 + i]))
            copies[-1].start()
    over = (((0,), (0,)), ((), ()))
    for t in range(2):
        for copy in copies[4 * t : 4 * t + 4]:
            copy.wait()
        at = slice(t * tile, (t + 1) * tile)
        acc = lax.dot_general(x_ref[...], s_ref[:, at], over, preferred_element_type=F32)
        out_ref[:, at] = acc.astype(BF)


def weight_grad(x_rows, parts, part, ff):
    rows, cols = x_rows.shape
    return call(
        functools.partial(weight_kernel, part),
        jax.ShapeDtypeStruct((cols, ff), BF),
        [VM] + [ANY] * 4,
        2 * cols * rows * ff,
        10 << 20,
        [pltpu.VMEM((rows, ff), BF), pltpu.SemaphoreType.DMA((8,))],
        18,
    )(x_rows, *parts)


def combine_kernel(ids_ref, *refs):
    pieces, out_ref = refs[:-1], refs[-1]
    hots = one_hot_slots(ids_ref[...])
    over = (((0,), (0,)), ((), ()))
    total = None
    for k in range(NX):
        d = (hots[k][0] + hots[k][1]).astype(BF)
        part = lax.dot_general(d, pieces[k][...], over, preferred_element_type=F32)
        total = part if total is None else total + part
    out_ref[...] = total.astype(BF)


def assemble_kernel(slab_ref, *refs):
    pieces, out_ref = refs[:-1], refs[-1]
    cols = pieces[0].shape[1]
    rows = 0
    for i, ref in enumerate(pieces):
        at = pl.multiple_of(slab_ref[min(i, 7)] * cols, 128)
        out_ref[rows : rows + ref.shape[0], pl.ds(at, cols)] = ref[...]
        rows = ref.shape[0] if i == 7 else 0


def call(kernel, out_shape, in_specs, flops=0, nbytes=0, scratch=(), mib=6):
    return pl.pallas_call(
        kernel,
        out_shape=out_shape,
        in_specs=in_specs,
        out_specs=jax.tree.map(lambda _: VM, out_shape),
        scratch_shapes=scratch,
        compiler_params=pltpu.CompilerParams(vmem_limit_bytes=mib << 20),
        cost_estimate=pl.CostEstimate(flops=flops, bytes_accessed=nbytes, transcendentals=0),
    )


def ring_sum(chunks, ties=((), (), (), ())):
    up, down, marks = chunks[4], chunks[5], []
    for i, o in enumerate((3, 2, 1, 0)):
        if ties[i]:
            up = after(up, *ties[i])
            down = after(down, *ties[i]) if i < 3 else down
        up = z_shift(up, 1)
        total = up.astype(F32) + chunks[o].astype(F32)
        if i < 2:
            down = z_shift(down, -1)
            down = (down.astype(F32) + chunks[9 - o].astype(F32)).astype(BF)
        elif i == 2:
            down = z_shift(down, -1)
        else:
            total = total + down.astype(F32)
        up = total.astype(BF)
        marks.append(up)
    return marks


def on_device(tokens, route_ids, route_weights, grad_gate, grad_up, gate_weight, up_weight):
    toks, width = tokens.shape
    cols, ff = gate_weight.shape
    dp, z = lax.axis_index("dp"), lax.axis_index("tp")
    x, y, c = dp // 8, dp // 2 % 4, dp % 2
    ids = lax.rem(route_ids.T - x + NX, NX)
    sent = call(
        dispatch_kernel,
        [jax.ShapeDtypeStruct((CAP, 2 * ff), BF)] * NX,
        [VM] * 4,
        2 * NX * CAP * toks * 2 * 2 * ff,
        4 << 20,
    )(ids, route_weights.T, grad_gate, grad_up)
    shifted = [sent[0]] + [x_shift(sent[k], k) for k in range(1, NX)]

    x_send = call(
        token_kernel,
        jax.ShapeDtypeStruct((32, CAP, cols), BF),
        [SM, VM, VM],
        2 * NX * CAP * toks * width,
        5 << 20,
        mib=10,
    )(x.reshape(1).astype(I32), ids, tokens)

    groups = ((0, 1), (2, 3))
    gate_other, up_other = c_swap(gate_weight), c_swap(up_weight)
    rows_a = jnp.concatenate([shifted[0], after(shifted[1], x_send, gate_other, up_other)], axis=0)
    up1_a, down1_a = y_shift(rows_a, 1), y_shift(rows_a, -1)
    rows_b = jnp.concatenate([shifted[2], shifted[3]], axis=0)
    half_up, half_down = up1_a[:, :ff], down1_a[:, ff:]
    rows_b = after(rows_b, half_up, half_down)
    up2_a, down2_a = y_shift(half_up, 1), y_shift(half_down, -1)
    up1_b, down1_b = y_shift(rows_b, 1), y_shift(rows_b, -1)

    place = jnp.stack([2 * j + (c + i) % 2 for i in range(2) for j in range(4)]).astype(I32)
    offset = lax.rem(place - z + NZ, NZ)
    n = 2 * CAP

    def product(where, *pieces):
        return call(
            partial_kernel,
            [jax.ShapeDtypeStruct((8, n, cols), BF), jax.ShapeDtypeStruct((4 * n, 2 * ff), BF)],
            [SM] + [VM] * 9,
            2 * 8 * n * 2 * ff * cols,
            12 << 20,
            mib=16,
        )(where, gate_weight, up_weight, gate_other, up_other, *pieces)

    chunks_a, s_a = product(after(offset, rows_b), rows_a, up1_a, down1_a, up2_a, down2_a)
    up1_b, down1_b = after(up1_b, chunks_a), after(down1_b, chunks_a)
    up2_b, down2_b = y_shift(up1_b[:, :ff], 1), y_shift(down1_b[:, ff:], -1)
    chunks_b, s_b = product(offset, rows_b, up1_b, down1_b, up2_b, down2_b)
    marks_a = ring_sum(chunks_a, ((), (up2_b, down2_b), (chunks_b,), ()))
    other_a = c_swap(after(s_a, marks_a[0]))
    other_b = c_swap(after(s_b, marks_a[2]))
    x_recv = lax.all_to_all(after(x_send, half_up), "dp", split_axis=0, concat_axis=0, tiled=True)
    order = jnp.stack(
        [
            (x - k) % NX * 8 + (y + j) % NY * 2 + (c + i) % 2
            for group in groups
            for i in range(2)
            for j in range(4)
            for k in group
        ]
    ).astype(I32)
    x_rows = call(
        rows_kernel,
        jax.ShapeDtypeStruct((32 * CAP, cols), BF),
        [SM, VM],
        0,
        7 << 20,
        mib=10,
    )(order, x_recv)
    marks_b = ring_sum(chunks_b, ((marks_a[1],), (marks_a[2], other_a), (marks_a[3], other_b, x_rows), ()))
    parts = [s_a, other_a, s_b, other_b]
    grad_gate_weight = weight_grad(x_rows, parts, 0, ff)
    grad_up_weight = weight_grad(x_rows, parts, 1, ff)
    back = []
    for group, summed in zip(groups, (marks_a[3], after(marks_b[3], grad_gate_weight))):
        for i, k in enumerate(group):
            back.append(give_back(summed[i * CAP : (i + 1) * CAP], k))
    back[-1] = after(back[-1], grad_up_weight)
    mine = call(
        combine_kernel, jax.ShapeDtypeStruct((toks, cols), BF), [VM] * 5, 2 * NX * CAP * toks * cols, 1 << 20
    )(ids, *back)

    back2, ahead2 = z_shift(mine, 2), z_shift(mine, -2)
    back1, ahead1 = z_shift(mine, 1), z_shift(mine, -1)
    back3, ahead3 = z_shift(back2, 1), z_shift(ahead2, -1)
    half = toks // 2
    top, bottom = z_shift(ahead2[:half], -2), z_shift(back2[half:], 2)
    got = [mine, back1, ahead1, back2, ahead2, back3, ahead3, top, bottom]
    slab = jnp.stack([(y - p // 2) % NY * 2 + p % 2 for p in [(z + d) % NZ for d in (0, -1, 1, -2, 2, -3, 3, -4)]])
    result = call(
        assemble_kernel,
        jax.ShapeDtypeStruct((toks, width), BF),
        [SM] + [VM] * 9,
        0,
        3 << 20,
    )(slab.astype(I32), *got)
    return (result, grad_gate_weight, grad_up_weight)


def solution(mesh):
    return jax.shard_map(
        on_device,
        mesh=mesh,
        in_specs=(
            P("dp", None),
            P("dp", None),
            P("dp", None),
            P("dp", None, "tp"),
            P("dp", None, "tp"),
            P("dp", "tp"),
            P("dp", "tp"),
        ),
        out_specs=(P("dp", None), P("dp", "tp"), P("dp", "tp")),
        check_vma=False,
    )
```

```python
import functools

import jax
import jax.numpy as jnp
from jax import lax
from jax.experimental import pallas as pl
from jax.experimental.pallas import tpu as pltpu
from jax.sharding import PartitionSpec as P

CAP = 72
NX, NY, NC, NZ = 4, 4, 2, 8
BF, F32, I32 = jnp.bfloat16, jnp.float32, jnp.int32
VM = pl.BlockSpec(memory_space=pltpu.VMEM)
SM = pl.BlockSpec(memory_space=pltpu.SMEM)
ANY = pl.BlockSpec(memory_space=pl.ANY)


def dp_perm(move):
    pairs = []
    for x in range(NX):
        for y in range(NY):
            for c in range(NC):
                tx, ty, tc = move(x, y, c)
                pairs.append(((x * NY + y) * NC + c, (tx % NX * NY + ty % NY) * NC + tc % NC))
    return pairs


def x_shift(value, k):
    return lax.ppermute(value, "dp", dp_perm(lambda x, y, c: (x + k, y, c)))


def y_shift(value, k):
    return lax.ppermute(value, "dp", dp_perm(lambda x, y, c: (x, y + k, c)))


def c_swap(value):
    return lax.ppermute(value, "dp", dp_perm(lambda x, y, c: (x, y, c + 1)))


def z_shift(value, k):
    return lax.ppermute(value, "tp", [(i, (i + k) % NZ) for i in range(NZ)])


def give_back(value, k):
    pairs = []
    for x in range(NX):
        for y in range(NY):
            for c in range(NC):
                for z in range(NZ):
                    to = ((x - k) % NX * NY + (y + z // 2) % NY) * NC + c
                    pairs.append((((x * NY + y) * NC + c) * NZ + z, to * NZ + z))
    return lax.ppermute(value, ("dp", "tp"), pairs)


def after(value, *others):
    return lax.optimization_barrier((value, *others))[0]


def one_hot_slots(ids):
    n = ids.shape[1]
    tri = (
        lax.broadcasted_iota(I32, (n, n), 0) < lax.broadcasted_iota(I32, (n, n), 1)
    ).astype(F32).astype(BF)
    rank = lax.broadcasted_iota(I32, (8, n), 0)
    hot0 = (rank == ids[0:1, :]).astype(F32)
    hot1 = (rank == ids[1:2, :]).astype(F32)
    pos0 = jnp.dot(hot0.astype(BF), tri, preferred_element_type=F32)
    pos1 = jnp.dot(hot1.astype(BF), tri, preferred_element_type=F32)
    pos1 = pos1 + jnp.sum(hot0, axis=1, keepdims=True)
    slot = lax.broadcasted_iota(I32, (CAP, n), 0)
    pairs = []
    for e in range(NX):
        at0 = jnp.where(hot0[e : e + 1, :] > 0.5, pos0[e : e + 1, :], -1.0).astype(I32)
        at1 = jnp.where(hot1[e : e + 1, :] > 0.5, pos1[e : e + 1, :], -1.0).astype(I32)
        pairs.append(((slot == at0).astype(F32), (slot == at1).astype(F32)))
    return pairs


def dispatch_kernel(ids_ref, w_ref, gg_ref, gu_ref, *out_refs):
    hots = one_hot_slots(ids_ref[...])
    w = w_ref[...].T
    ff = gg_ref.shape[2]
    for part, ref in enumerate((gg_ref, gu_ref)):
        s0 = (ref[:, 0, :].astype(F32) * w[:, 0:1]).astype(BF)
        s1 = (ref[:, 1, :].astype(F32) * w[:, 1:2]).astype(BF)
        for e in range(NX):
            d0, d1 = hots[e]
            rows = jnp.dot(d0.astype(BF), s0, preferred_element_type=F32)
            rows = rows + jnp.dot(d1.astype(BF), s1, preferred_element_type=F32)
            out_refs[e][:, part * ff : (part + 1) * ff] = rows.astype(BF)


def token_kernel(x_ref, ids_ref, tok_ref, out_ref):
    hots = one_hot_slots(ids_ref[...])
    slabs = NY * NC
    cols = tok_ref.shape[1] // slabs
    for k in range(NX):
        d = (hots[k][0] + hots[k][1]).astype(BF)
        base = lax.rem(x_ref[0] + k, NX) * slabs
        for g in range(slabs):
            rows = jnp.dot(d, tok_ref[:, g * cols : (g + 1) * cols], preferred_element_type=F32)
            out_ref[base + g] = rows.astype(BF)


def partial_kernel(o_ref, go_ref, uo_ref, gs_ref, us_ref, own, up1, down1, up2, down2, p_ref, s_ref):
    ff = go_ref.shape[1]
    n = p_ref.shape[1]
    s_ref[0:n, :] = own[...]
    s_ref[n : 2 * n, :] = down1[...]
    s_ref[2 * n : 3 * n, 0:ff] = up2[...]
    s_ref[2 * n : 3 * n, ff:] = down2[...]
    s_ref[3 * n :, :] = up1[...]
    over = (((1,), (1,)), ((), ()))
    for which, (g_ref, u_ref) in enumerate(((go_ref, uo_ref), (gs_ref, us_ref))):
        acc = lax.dot_general(s_ref[:, 0:ff], g_ref[...], over, preferred_element_type=F32)
        acc = acc + lax.dot_general(s_ref[:, ff:], u_ref[...], over, preferred_element_type=F32)
        for j in range(4):
            p_ref[o_ref[which * 4 + j]] = acc[j * n : (j + 1) * n, :].astype(BF)


def rows_kernel(order_ref, x_ref, xs_ref):
    cap = x_ref.shape[1]

    def put(m, _):
        pair = [x_ref[order_ref[2 * m + i]].astype(F32) for i in range(2)]
        rows = pl.ds(pl.multiple_of(m * (2 * cap), 16), 2 * cap)
        xs_ref[rows, :] = jnp.concatenate(pair, axis=0).astype(BF)
        return 0

    lax.fori_loop(0, x_ref.shape[0] // 2, put, 0)


def weight_kernel(part, x_ref, sa, sb, sc, sd, out_ref, s_ref, sems):
    ff = out_ref.shape[1]
    n = sa.shape[0]
    tile = ff // 2
    copies = []
    for t in range(2):
        for i, ref in enumerate((sa, sb, sc, sd)):
            src = ref.at[:, pl.ds(part * ff + t * tile, tile)]
            dst = s_ref.at[pl.ds(i * n, n), pl.ds(t * tile, tile)]
            copies.append(pltpu.make_async_copy(src, dst, sems.at[t * 4 + i]))
            copies[-1].start()
    over = (((0,), (0,)), ((), ()))
    for t in range(2):
        for copy in copies[4 * t : 4 * t + 4]:
            copy.wait()
        at = slice(t * tile, (t + 1) * tile)
        acc = lax.dot_general(x_ref[...], s_ref[:, at], over, preferred_element_type=F32)
        out_ref[:, at] = acc.astype(BF)


def weight_grad(x_rows, parts, part, ff):
    rows, cols = x_rows.shape
    return call(
        functools.partial(weight_kernel, part),
        jax.ShapeDtypeStruct((cols, ff), BF),
        [VM] + [ANY] * 4,
        2 * cols * rows * ff,
        10 << 20,
        [pltpu.VMEM((rows, ff), BF), pltpu.SemaphoreType.DMA((8,))],
        18,
    )(x_rows, *parts)


def combine_kernel(ids_ref, *refs):
    pieces, out_ref = refs[:-1], refs[-1]
    hots = one_hot_slots(ids_ref[...])
    over = (((0,), (0,)), ((), ()))
    total = None
    for k in range(NX):
        d = (hots[k][0] + hots[k][1]).astype(BF)
        part = lax.dot_general(d, pieces[k][...], over, preferred_element_type=F32)
        total = part if total is None else total + part
    out_ref[...] = total.astype(BF)


def assemble_kernel(slab_ref, *refs):
    pieces, out_ref = refs[:-1], refs[-1]
    cols = pieces[0].shape[1]
    rows = 0
    for i, ref in enumerate(pieces):
        at = pl.multiple_of(slab_ref[min(i, 7)] * cols, 128)
        out_ref[rows : rows + ref.shape[0], pl.ds(at, cols)] = ref[...]
        rows = ref.shape[0] if i == 7 else 0


def call(kernel, out_shape, in_specs, flops=0, nbytes=0, scratch=(), mib=6):
    return pl.pallas_call(
        kernel,
        out_shape=out_shape,
        in_specs=in_specs,
        out_specs=jax.tree.map(lambda _: VM, out_shape),
        scratch_shapes=scratch,
        compiler_params=pltpu.CompilerParams(vmem_limit_bytes=mib << 20),
        cost_estimate=pl.CostEstimate(flops=flops, bytes_accessed=nbytes, transcendentals=0),
    )


def ring_sum(chunks, ties=((), (), (), ())):
    up, down, marks = chunks[4], chunks[5], []
    for i, o in enumerate((3, 2, 1, 0)):
        if ties[i]:
            up = after(up, *ties[i])
            down = after(down, *ties[i]) if i < 3 else down
        up = z_shift(up, 1)
        total = up.astype(F32) + chunks[o].astype(F32)
        if i < 2:
            down = z_shift(down, -1)
            down = (down.astype(F32) + chunks[9 - o].astype(F32)).astype(BF)
        elif i == 2:
            down = z_shift(down, -1)
        else:
            total = total + down.astype(F32)
        up = total.astype(BF)
        marks.append(up)
    return marks


def two_stage_sum(chunks, first, second):
    half = chunks.shape[1] // 2
    held = [after(chunks[o], *first) for o in (3, 4, 5)]
    a, b = z_shift(held[0], 1), z_shift(held[2], -1)
    top, low = z_shift(held[1][:half], 2), z_shift(held[1][half:], -2)
    a = chunks[2].astype(F32) + a.astype(F32)
    b = chunks[6].astype(F32) + b.astype(F32)
    a = jnp.concatenate([a[:half] + top.astype(F32), a[half:]], axis=0).astype(BF)
    b = jnp.concatenate([b[:half], b[half:] + low.astype(F32)], axis=0).astype(BF)
    a, b = after(a, *second), after(b, *second)
    far = [z_shift(a, 2), z_shift(b, -2), z_shift(chunks[1], 1), z_shift(chunks[7], -1)]
    total = chunks[0].astype(F32)
    for value in far:
        total = total + value.astype(F32)
    return total.astype(BF)


def on_device(tokens, route_ids, route_weights, grad_gate, grad_up, gate_weight, up_weight):
    toks, width = tokens.shape
    cols, ff = gate_weight.shape
    dp, z = lax.axis_index("dp"), lax.axis_index("tp")
    x, y, c = dp // 8, dp // 2 % 4, dp % 2
    ids = lax.rem(route_ids.T - x + NX, NX)
    sent = call(
        dispatch_kernel,
        [jax.ShapeDtypeStruct((CAP, 2 * ff), BF)] * NX,
        [VM] * 4,
        2 * NX * CAP * toks * 2 * 2 * ff,
        4 << 20,
    )(ids, route_weights.T, grad_gate, grad_up)
    shifted = [sent[0]] + [x_shift(sent[k], k) for k in range(1, NX)]

    x_send = call(
        token_kernel,
        jax.ShapeDtypeStruct((32, CAP, cols), BF),
        [SM, VM, VM],
        2 * NX * CAP * toks * width,
        5 << 20,
        mib=10,
    )(x.reshape(1).astype(I32), ids, tokens)

    groups = ((0, 1), (2, 3))
    gate_other, up_other = c_swap(gate_weight), c_swap(up_weight)
    rows_a = jnp.concatenate([shifted[0], after(shifted[1], x_send, gate_other, up_other)], axis=0)
    up1_a, down1_a = y_shift(rows_a, 1), y_shift(rows_a, -1)
    rows_b = jnp.concatenate([shifted[2], shifted[3]], axis=0)
    half_up, half_down = up1_a[:, :ff], down1_a[:, ff:]
    rows_b = after(rows_b, half_up, half_down)
    up2_a, down2_a = y_shift(half_up, 1), y_shift(half_down, -1)
    up1_b, down1_b = y_shift(rows_b, 1), y_shift(rows_b, -1)

    place = jnp.stack([2 * j + (c + i) % 2 for i in range(2) for j in range(4)]).astype(I32)
    offset = lax.rem(place - z + NZ, NZ)
    n = 2 * CAP

    def product(where, *pieces):
        return call(
            partial_kernel,
            [jax.ShapeDtypeStruct((8, n, cols), BF), jax.ShapeDtypeStruct((4 * n, 2 * ff), BF)],
            [SM] + [VM] * 9,
            2 * 8 * n * 2 * ff * cols,
            12 << 20,
            mib=16,
        )(where, gate_weight, up_weight, gate_other, up_other, *pieces)

    chunks_a, s_a = product(after(offset, rows_b), rows_a, up1_a, down1_a, up2_a, down2_a)
    up1_b, down1_b = after(up1_b, chunks_a), after(down1_b, chunks_a)
    up2_b, down2_b = y_shift(up1_b[:, :ff], 1), y_shift(down1_b[:, ff:], -1)
    chunks_b, s_b = product(offset, rows_b, up1_b, down1_b, up2_b, down2_b)
    marks_a = ring_sum(chunks_a, ((), (up2_b, down2_b), (chunks_b,), ()))
    other_a = c_swap(after(s_a, marks_a[0]))
    other_b = c_swap(after(s_b, marks_a[2]))
    x_recv = lax.all_to_all(after(x_send, half_up), "dp", split_axis=0, concat_axis=0, tiled=True)
    order = jnp.stack(
        [
            (x - k) % NX * 8 + (y + j) % NY * 2 + (c + i) % 2
            for group in groups
            for i in range(2)
            for j in range(4)
            for k in group
        ]
    ).astype(I32)
    x_rows = call(
        rows_kernel,
        jax.ShapeDtypeStruct((32 * CAP, cols), BF),
        [SM, VM],
        0,
        7 << 20,
        mib=10,
    )(order, x_recv)
    sum_b = two_stage_sum(chunks_b, (marks_a[1],), (marks_a[3], other_a, other_b, x_rows))
    parts = [s_a, other_a, s_b, other_b]
    grad_gate_weight = weight_grad(x_rows, parts, 0, ff)
    grad_up_weight = weight_grad(x_rows, parts, 1, ff)
    back = []
    for group, summed in zip(groups, (marks_a[3], after(sum_b, grad_gate_weight))):
        for i, k in enumerate(group):
            back.append(give_back(summed[i * CAP : (i + 1) * CAP], k))
    back[-1] = after(back[-1], grad_up_weight)
    mine = call(
        combine_kernel, jax.ShapeDtypeStruct((toks, cols), BF), [VM] * 5, 2 * NX * CAP * toks * cols, 1 << 20
    )(ids, *back)

    back2, ahead2 = z_shift(mine, 2), z_shift(mine, -2)
    back1, ahead1 = z_shift(mine, 1), z_shift(mine, -1)
    back3, ahead3 = z_shift(back2, 1), z_shift(ahead2, -1)
    half = toks // 2
    top, bottom = z_shift(ahead2[:half], -2), z_shift(back2[half:], 2)
    got = [mine, back1, ahead1, back2, ahead2, back3, ahead3, top, bottom]
    slab = jnp.stack([(y - p // 2) % NY * 2 + p % 2 for p in [(z + d) % NZ for d in (0, -1, 1, -2, 2, -3, 3, -4)]])
    result = call(
        assemble_kernel,
        jax.ShapeDtypeStruct((toks, width), BF),
        [SM] + [VM] * 9,
        0,
        3 << 20,
    )(slab.astype(I32), *got)
    return (result, grad_gate_weight, grad_up_weight)


def solution(mesh):
    return jax.shard_map(
        on_device,
        mesh=mesh,
        in_specs=(
            P("dp", None),
            P("dp", None),
            P("dp", None),
            P("dp", None, "tp"),
            P("dp", None, "tp"),
            P("dp", "tp"),
            P("dp", "tp"),
        ),
        out_specs=(P("dp", None), P("dp", "tp"), P("dp", "tp")),
        check_vma=False,
    )
```

```python
import functools

import jax
import jax.numpy as jnp
from jax import lax
from jax.experimental import pallas as pl
from jax.experimental.pallas import tpu as pltpu
from jax.sharding import PartitionSpec as P

CAP = 72
NX, NY, NC, NZ = 4, 4, 2, 8
BF, F32, I32 = jnp.bfloat16, jnp.float32, jnp.int32
VM = pl.BlockSpec(memory_space=pltpu.VMEM)
SM = pl.BlockSpec(memory_space=pltpu.SMEM)
ANY = pl.BlockSpec(memory_space=pl.ANY)


def dp_perm(move):
    pairs = []
    for x in range(NX):
        for y in range(NY):
            for c in range(NC):
                tx, ty, tc = move(x, y, c)
                pairs.append(((x * NY + y) * NC + c, (tx % NX * NY + ty % NY) * NC + tc % NC))
    return pairs


def x_shift(value, k):
    return lax.ppermute(value, "dp", dp_perm(lambda x, y, c: (x + k, y, c)))


def y_shift(value, k):
    return lax.ppermute(value, "dp", dp_perm(lambda x, y, c: (x, y + k, c)))


def c_swap(value):
    return lax.ppermute(value, "dp", dp_perm(lambda x, y, c: (x, y, c + 1)))


def z_shift(value, k):
    return lax.ppermute(value, "tp", [(i, (i + k) % NZ) for i in range(NZ)])


def give_back(value, k):
    pairs = []
    for x in range(NX):
        for y in range(NY):
            for c in range(NC):
                for z in range(NZ):
                    to = ((x - k) % NX * NY + (y + z // 2) % NY) * NC + c
                    pairs.append((((x * NY + y) * NC + c) * NZ + z, to * NZ + z))
    return lax.ppermute(value, ("dp", "tp"), pairs)


def after(value, *others):
    return lax.optimization_barrier((value, *others))[0]


def one_hot_slots(ids):
    n = ids.shape[1]
    tri = (
        lax.broadcasted_iota(I32, (n, n), 0) < lax.broadcasted_iota(I32, (n, n), 1)
    ).astype(F32).astype(BF)
    rank = lax.broadcasted_iota(I32, (8, n), 0)
    hot0 = (rank == ids[0:1, :]).astype(F32)
    hot1 = (rank == ids[1:2, :]).astype(F32)
    pos0 = jnp.dot(hot0.astype(BF), tri, preferred_element_type=F32)
    pos1 = jnp.dot(hot1.astype(BF), tri, preferred_element_type=F32)
    pos1 = pos1 + jnp.sum(hot0, axis=1, keepdims=True)
    slot = lax.broadcasted_iota(I32, (CAP, n), 0)
    pairs = []
    for e in range(NX):
        at0 = jnp.where(hot0[e : e + 1, :] > 0.5, pos0[e : e + 1, :], -1.0).astype(I32)
        at1 = jnp.where(hot1[e : e + 1, :] > 0.5, pos1[e : e + 1, :], -1.0).astype(I32)
        pairs.append(((slot == at0).astype(F32), (slot == at1).astype(F32)))
    return pairs


def dispatch_kernel(ids_ref, w_ref, gg_ref, gu_ref, *out_refs):
    hots = one_hot_slots(ids_ref[...])
    w = w_ref[...].T
    ff = gg_ref.shape[2]
    for part, ref in enumerate((gg_ref, gu_ref)):
        s0 = (ref[:, 0, :].astype(F32) * w[:, 0:1]).astype(BF)
        s1 = (ref[:, 1, :].astype(F32) * w[:, 1:2]).astype(BF)
        for e in range(NX):
            d0, d1 = hots[e]
            rows = jnp.dot(d0.astype(BF), s0, preferred_element_type=F32)
            rows = rows + jnp.dot(d1.astype(BF), s1, preferred_element_type=F32)
            out_refs[e][:, part * ff : (part + 1) * ff] = rows.astype(BF)


def token_kernel(x_ref, ids_ref, tok_ref, out_ref):
    hots = one_hot_slots(ids_ref[...])
    slabs = NY * NC
    cols = tok_ref.shape[1] // slabs
    for k in range(NX):
        d = (hots[k][0] + hots[k][1]).astype(BF)
        base = lax.rem(x_ref[0] + k, NX) * slabs
        for g in range(slabs):
            rows = jnp.dot(d, tok_ref[:, g * cols : (g + 1) * cols], preferred_element_type=F32)
            out_ref[base + g] = rows.astype(BF)


def partial_kernel(o_ref, go_ref, uo_ref, gs_ref, us_ref, own, up1, down1, up2, down2, p_ref, s_ref):
    ff = go_ref.shape[1]
    n = p_ref.shape[1]
    s_ref[0:n, :] = own[...]
    s_ref[n : 2 * n, :] = down1[...]
    s_ref[2 * n : 3 * n, 0:ff] = up2[...]
    s_ref[2 * n : 3 * n, ff:] = down2[...]
    s_ref[3 * n :, :] = up1[...]
    over = (((1,), (1,)), ((), ()))
    for which, (g_ref, u_ref) in enumerate(((go_ref, uo_ref), (gs_ref, us_ref))):
        acc = lax.dot_general(s_ref[:, 0:ff], g_ref[...], over, preferred_element_type=F32)
        acc = acc + lax.dot_general(s_ref[:, ff:], u_ref[...], over, preferred_element_type=F32)
        for j in range(4):
            p_ref[o_ref[which * 4 + j]] = acc[j * n : (j + 1) * n, :].astype(BF)


def rows_kernel(order_ref, x_ref, xs_ref):
    cap = x_ref.shape[1]

    def put(m, _):
        pair = [x_ref[order_ref[2 * m + i]].astype(F32) for i in range(2)]
        rows = pl.ds(pl.multiple_of(m * (2 * cap), 16), 2 * cap)
        xs_ref[rows, :] = jnp.concatenate(pair, axis=0).astype(BF)
        return 0

    lax.fori_loop(0, x_ref.shape[0] // 2, put, 0)


def weight_kernel(part, x_ref, sa, sb, sc, sd, out_ref, s_ref, sems):
    ff = out_ref.shape[1]
    n = sa.shape[0]
    tile = ff // 2
    copies = []
    for t in range(2):
        for i, ref in enumerate((sa, sb, sc, sd)):
            src = ref.at[:, pl.ds(part * ff + t * tile, tile)]
            dst = s_ref.at[pl.ds(i * n, n), pl.ds(t * tile, tile)]
            copies.append(pltpu.make_async_copy(src, dst, sems.at[t * 4 + i]))
            copies[-1].start()
    over = (((0,), (0,)), ((), ()))
    for t in range(2):
        for copy in copies[4 * t : 4 * t + 4]:
            copy.wait()
        at = slice(t * tile, (t + 1) * tile)
        acc = lax.dot_general(x_ref[...], s_ref[:, at], over, preferred_element_type=F32)
        out_ref[:, at] = acc.astype(BF)


def weight_grad(x_rows, parts, part, ff):
    rows, cols = x_rows.shape
    return call(
        functools.partial(weight_kernel, part),
        jax.ShapeDtypeStruct((cols, ff), BF),
        [VM] + [ANY] * 4,
        2 * cols * rows * ff,
        10 << 20,
        [pltpu.VMEM((rows, ff), BF), pltpu.SemaphoreType.DMA((8,))],
        18,
    )(x_rows, *parts)


def combine_kernel(ids_ref, *refs):
    pieces, out_ref = refs[:-1], refs[-1]
    hots = one_hot_slots(ids_ref[...])
    over = (((0,), (0,)), ((), ()))
    total = None
    for k in range(NX):
        d = (hots[k][0] + hots[k][1]).astype(BF)
        part = lax.dot_general(d, pieces[k][...], over, preferred_element_type=F32)
        total = part if total is None else total + part
    out_ref[...] = total.astype(BF)


def assemble_kernel(slab_ref, *refs):
    pieces, out_ref = refs[:-1], refs[-1]
    cols = pieces[0].shape[1]
    rows = 0
    for i, ref in enumerate(pieces):
        at = pl.multiple_of(slab_ref[min(i, 7)] * cols, 128)
        out_ref[rows : rows + ref.shape[0], pl.ds(at, cols)] = ref[...]
        rows = ref.shape[0] if i == 7 else 0


def call(kernel, out_shape, in_specs, flops=0, nbytes=0, scratch=(), mib=6):
    return pl.pallas_call(
        kernel,
        out_shape=out_shape,
        in_specs=in_specs,
        out_specs=jax.tree.map(lambda _: VM, out_shape),
        scratch_shapes=scratch,
        compiler_params=pltpu.CompilerParams(vmem_limit_bytes=mib << 20),
        cost_estimate=pl.CostEstimate(flops=flops, bytes_accessed=nbytes, transcendentals=0),
    )


def ring_sum(chunks, ties=((), (), (), ())):
    up, down, marks = chunks[4], chunks[5], []
    for i, o in enumerate((3, 2, 1, 0)):
        if ties[i]:
            up = after(up, *ties[i])
            down = after(down, *ties[i]) if i < 3 else down
        up = z_shift(up, 1)
        total = up.astype(F32) + chunks[o].astype(F32)
        if i < 2:
            down = z_shift(down, -1)
            down = (down.astype(F32) + chunks[9 - o].astype(F32)).astype(BF)
        elif i == 2:
            down = z_shift(down, -1)
        else:
            total = total + down.astype(F32)
        up = total.astype(BF)
        marks.append(up)
    return marks


def two_stage_sum(chunks, first, second):
    half = chunks.shape[1] // 2
    held = [after(chunks[o], *first) for o in (3, 4, 5)]
    a, b = z_shift(held[0], 1), z_shift(held[2], -1)
    top, low = z_shift(held[1][:half], 2), z_shift(held[1][half:], -2)
    a = chunks[2].astype(F32) + a.astype(F32)
    b = chunks[6].astype(F32) + b.astype(F32)
    a = jnp.concatenate([a[:half] + top.astype(F32), a[half:]], axis=0).astype(BF)
    b = jnp.concatenate([b[:half], b[half:] + low.astype(F32)], axis=0).astype(BF)
    a, b = after(a, *second), after(b, *second)
    far = [z_shift(a, 2), z_shift(b, -2), z_shift(chunks[1], 1), z_shift(chunks[7], -1)]
    total = chunks[0].astype(F32)
    for value in far:
        total = total + value.astype(F32)
    return total.astype(BF)


def on_device(tokens, route_ids, route_weights, grad_gate, grad_up, gate_weight, up_weight):
    toks, width = tokens.shape
    cols, ff = gate_weight.shape
    dp, z = lax.axis_index("dp"), lax.axis_index("tp")
    x, y, c = dp // 8, dp // 2 % 4, dp % 2
    ids = lax.rem(route_ids.T - x + NX, NX)
    sent = call(
        dispatch_kernel,
        [jax.ShapeDtypeStruct((CAP, 2 * ff), BF)] * NX,
        [VM] * 4,
        2 * NX * CAP * toks * 2 * 2 * ff,
        4 << 20,
    )(ids, route_weights.T, grad_gate, grad_up)
    shifted = [sent[0]] + [x_shift(sent[k], k) for k in range(1, NX)]

    x_send = call(
        token_kernel,
        jax.ShapeDtypeStruct((32, CAP, cols), BF),
        [SM, VM, VM],
        2 * NX * CAP * toks * width,
        5 << 20,
        mib=10,
    )(x.reshape(1).astype(I32), ids, tokens)

    groups = ((0, 1), (2, 3))
    gate_other, up_other = c_swap(gate_weight), c_swap(up_weight)
    rows_a = jnp.concatenate([shifted[0], after(shifted[1], x_send, gate_other, up_other)], axis=0)
    up1_a, down1_a = y_shift(rows_a, 1), y_shift(rows_a, -1)
    rows_b = jnp.concatenate([shifted[2], shifted[3]], axis=0)
    half_up, half_down = up1_a[:, :ff], down1_a[:, ff:]
    rows_b = after(rows_b, half_up, half_down)
    up2_a, down2_a = y_shift(half_up, 1), y_shift(half_down, -1)
    up1_b, down1_b = y_shift(rows_b, 1), y_shift(rows_b, -1)

    place = jnp.stack([2 * j + (c + i) % 2 for i in range(2) for j in range(4)]).astype(I32)
    offset = lax.rem(place - z + NZ, NZ)
    n = 2 * CAP

    def product(where, *pieces):
        return call(
            partial_kernel,
            [jax.ShapeDtypeStruct((8, n, cols), BF), jax.ShapeDtypeStruct((4 * n, 2 * ff), BF)],
            [SM] + [VM] * 9,
            2 * 8 * n * 2 * ff * cols,
            12 << 20,
            mib=16,
        )(where, gate_weight, up_weight, gate_other, up_other, *pieces)

    chunks_a, s_a = product(after(offset, rows_b), rows_a, up1_a, down1_a, up2_a, down2_a)
    up1_b, down1_b = after(up1_b, chunks_a), after(down1_b, chunks_a)
    up2_b, down2_b = y_shift(up1_b[:, :ff], 1), y_shift(down1_b[:, ff:], -1)
    chunks_b, s_b = product(offset, rows_b, up1_b, down1_b, up2_b, down2_b)
    marks_a = ring_sum(chunks_a, ((), (up2_b, down2_b), (chunks_b,), ()))
    other_a = c_swap(after(s_a, marks_a[0]))
    other_b = c_swap(after(s_b, marks_a[2]))
    x_recv = lax.all_to_all(after(x_send, half_up), "dp", split_axis=0, concat_axis=0, tiled=True)
    order = jnp.stack(
        [
            (x - k) % NX * 8 + (y + j) % NY * 2 + (c + i) % 2
            for group in groups
            for i in range(2)
            for j in range(4)
            for k in group
        ]
    ).astype(I32)
    x_rows = call(
        rows_kernel,
        jax.ShapeDtypeStruct((32 * CAP, cols), BF),
        [SM, VM],
        0,
        7 << 20,
        mib=10,
    )(order, x_recv)
    sum_b = two_stage_sum(chunks_b, (marks_a[1],), (other_a, other_b))
    parts = [s_a, other_a, s_b, other_b]
    grad_gate_weight = weight_grad(x_rows, parts, 0, ff)
    grad_up_weight = weight_grad(x_rows, parts, 1, ff)
    back = []
    for group, summed in zip(groups, (marks_a[3], after(sum_b, grad_gate_weight))):
        for i, k in enumerate(group):
            back.append(give_back(summed[i * CAP : (i + 1) * CAP], k))
    back[-1] = after(back[-1], grad_up_weight)
    mine = call(
        combine_kernel, jax.ShapeDtypeStruct((toks, cols), BF), [VM] * 5, 2 * NX * CAP * toks * cols, 1 << 20
    )(ids, *back)

    back2, ahead2 = z_shift(mine, 2), z_shift(mine, -2)
    back1, ahead1 = z_shift(mine, 1), z_shift(mine, -1)
    back3, ahead3 = z_shift(back2, 1), z_shift(ahead2, -1)
    half = toks // 2
    top, bottom = z_shift(ahead2[:half], -2), z_shift(back2[half:], 2)
    got = [mine, back1, ahead1, back2, ahead2, back3, ahead3, top, bottom]
    slab = jnp.stack([(y - p // 2) % NY * 2 + p % 2 for p in [(z + d) % NZ for d in (0, -1, 1, -2, 2, -3, 3, -4)]])
    result = call(
        assemble_kernel,
        jax.ShapeDtypeStruct((toks, width), BF),
        [SM] + [VM] * 9,
        0,
        3 << 20,
    )(slab.astype(I32), *got)
    return (result, grad_gate_weight, grad_up_weight)


def solution(mesh):
    return jax.shard_map(
        on_device,
        mesh=mesh,
        in_specs=(
            P("dp", None),
            P("dp", None),
            P("dp", None),
            P("dp", None, "tp"),
            P("dp", None, "tp"),
            P("dp", "tp"),
            P("dp", "tp"),
        ),
        out_specs=(P("dp", None), P("dp", "tp"), P("dp", "tp")),
        check_vma=False,
    )
```
